32 devices in a mesh: fsdp: 16 (over z, x, core), dp: 2 (over y).
Axes of the slice: x: 2, y: 2, z: 4, core: 2. Of those that a mesh axis runs over, the one named last changes fastest.
Arguments:
- activations: bfloat16 [8192, 4096], P(('fsdp', 'dp')), may hold values from -6 to 6
- cotangents: bfloat16 [2, 8192, 4096], P(None, ('fsdp', 'dp')), may hold values from -6 to 6
- weights: bfloat16 [2, 4096, 4096], P(None, 'fsdp'), may hold values from -4 to 4
- projectors: bfloat16 [2, 4096, 512], P(None, 'fsdp'), may hold values from -0.09375 to 0.09375
- first_moment: float32 [2, 4096, 512], P(None, 'fsdp'), may hold values from -3 to 3
- second_moment: float32 [2, 4096, 512], P(None, 'fsdp'), may hold values from 0.25 to 4
- matrix_settings: int32 [2, 2], replicated, may hold values from 0 to 512, as said below
Outputs:
- new_weights: bfloat16 [2, 4096, 4096], P(None, 'fsdp')
- new_first: float32 [2, 4096, 512], P(None, 'fsdp')
- new_second: float32 [2, 4096, 512], P(None, 'fsdp')
The draws below stay inside these ranges and needn't reach their ends.
Inputs may be any that keep to these rules, and one draw needn't show every extreme that they name: `matrix_settings`: column 0 is a rank from 128 to 512, some matrix has rank exactly 512; column 1 is 0 (the projector acts on the activations) or 1 (on the cotangents), and both values occur.
All inputs are finite; a program needn't handle non-finite values.
Results may differ from the reference program's by a relative error of at most 0.0045.
Values may be sent and summed in bfloat16 or wider, within the bound.
A program may use at most 128 MiB of HBM per device.

```python
import math
import jax
import jax.numpy as jnp
from jax import lax

D = 4096
MATS = 2
RMAX = 512
TOKENS = 8192


def draw_matrix_settings(key, part):
    first_key, second_key = jax.random.split(jax.random.fold_in(key, 17))
    drawn = jax.random.randint(first_key, (MATS,), RMAX // 4, RMAX + 1)
    chosen = jax.random.randint(second_key, (), 0, MATS)
    ranks = jnp.where(jnp.arange(MATS) == chosen, RMAX, drawn)
    offset = jax.random.randint(jax.random.fold_in(key, 29), (), 0, 2)
    sides = (jnp.arange(MATS) + offset) % 2
    return jnp.stack([ranks, sides], axis=1).astype(jnp.int32)


def level_of(stream_key, dims, cuts, low, largest):
    loudness, own = 1.0, jax.random.fold_in(stream_key, 6)
    for position, blocks in cuts:
        steps = jnp.exp(jax.random.uniform(jax.random.fold_in(own, position), (blocks,), jnp.float32, low / len(cuts), largest / len(cuts)))
        loudness = loudness * jnp.repeat(steps, dims[position] // blocks).reshape([-1 if axis == position else 1 for axis in range(len(dims))])
    return loudness


def scatter_about(rng, extent, width, bound, cuts=(), held_as=jnp.bfloat16):
    values = width * jax.random.normal(rng, extent, jnp.float32)
    if cuts:
        values = values * level_of(rng, extent, cuts, -0.22, 0.18)
    return jnp.clip(values, -bound, bound).astype(held_as)


def setup_inputs(seed: int = 0) -> dict:
    key_of = jax.random.split(jax.random.key(seed), 8)
    return {
        "activations": scatter_about(key_of[0], (TOKENS, D), 1.0, 6.0, ((0, 32),)),
        "cotangents": scatter_about(key_of[1], (MATS, TOKENS, D), 1.0, 6.0, ((1, 32),)),
        "weights": scatter_about(key_of[2], (MATS, D, D), 0.5, 4.0, ((1, 16),)),
        "projectors": scatter_about(key_of[3], (MATS, D, RMAX), D ** -0.5, 0.09375, ((1, 16),)),
        "first_moment": scatter_about(key_of[4], (MATS, D, RMAX), 0.5, 3.0, ((1, 16),), jnp.float32),
        "second_moment": jnp.clip(jnp.exp(math.log(4.0) - 2.7725887 * jax.random.uniform(key_of[5], (MATS, D, RMAX), jnp.float32) ** level_of(key_of[5], (MATS, D, RMAX), ((1, 16),), -0.2, 0.2)), 0.25, 4.0),
        "matrix_settings": draw_matrix_settings(jax.random.fold_in(key_of[7], 71), 0),
    }


BETA_ONE = 0.9
BETA_TWO = 0.95
EPSILON = 1e-08

def contract_tokens(left_operand, right_operand):
    return lax.dot_general(left_operand, right_operand, (((0,), (0,)), ((), ())), preferred_element_type=jnp.float32)

def reference(activations, cotangents, weights, projectors, first_moment, second_moment, matrix_settings):
    grad_scale = 1.0 / math.sqrt(activations.shape[0])
    rank_columns = jnp.arange(projectors.shape[2])
    weight_list, first_list, second_list = ([], [], [])
    for matrix_index in range(cotangents.shape[0]):
        live_mask = (rank_columns < matrix_settings[matrix_index, 0])[None, :]
        on_inputs = matrix_settings[matrix_index, 1] == 0
        projector = jnp.where(live_mask, projectors[matrix_index], jnp.zeros((), projectors.dtype))
        grads_out = cotangents[matrix_index]
        coeffs = lax.cond(on_inputs, lambda: jnp.dot(activations, projector, preferred_element_type=jnp.float32), lambda: jnp.dot(grads_out, projector, preferred_element_type=jnp.float32)).astype(jnp.bfloat16)
        projected = lax.cond(on_inputs, lambda: contract_tokens(grads_out, coeffs), lambda: contract_tokens(activations, coeffs)) * grad_scale
        moment_one = jnp.where(live_mask, BETA_ONE * first_moment[matrix_index] + (1.0 - BETA_ONE) * projected, 0.0)
        moment_two = jnp.where(live_mask, BETA_TWO * second_moment[matrix_index] + (1.0 - BETA_TWO) * projected * projected, 0.0)
        normalized = jnp.where(live_mask, moment_one / (jnp.sqrt(moment_two) + EPSILON), 0.0).astype(jnp.bfloat16)
        update = lax.dot_general(normalized, projector, (((1,), (1,)), ((), ())), preferred_element_type=jnp.float32)
        weight_list.append((weights[matrix_index].astype(jnp.float32) - update).astype(jnp.bfloat16))
        first_list.append(moment_one)
        second_list.append(moment_two)
    return (jnp.stack(weight_list), jnp.stack(first_list), jnp.stack(second_list))
```

```python
import functools
import math

import jax
import jax.numpy as jnp
from jax import lax
from jax.experimental import pallas as pl
from jax.experimental.pallas import tpu as pltpu
from jax.sharding import PartitionSpec as P

BETA_ONE = 0.9
BETA_TWO = 0.95
EPSILON = 1e-08
MESH = pl.DeviceIdType.MESH
BF16, F32 = jnp.bfloat16, jnp.float32


def split_axis(fsdp):
    chips = fsdp // 2
    inner = 1
    while (2 * inner) ** 2 <= chips and chips % (2 * inner) == 0:
        inner *= 2
    return chips // inner, inner


def shared_rows(rows, dp):
    return (rows * 3 // 8) // 32 * 32 if dp == 2 else 0


def kernel(
    fsdp, dp, scale,
    settings, act, cot, wts, prj, mom1, mom2, w_out, m1_out, m2_out,
    xs, proj, own_t, sib_t, send_t, own_c, sib_c, acc, zacc, xsend, xrecv, zsend, zrecv, ybuf, wbuf, m1, m2, nbuf,
    in_sem, out_sem, gz, gx, gy, gs, st, sc, rx, rz, ry,
):
    mats, _, rows, rank_max = proj.shape
    tokens = act.shape[0]
    outer, inner = split_axis(fsdp)
    chips = outer * inner
    me, my_dp = lax.axis_index("fsdp"), lax.axis_index("dp")
    core = lax.rem(me, 2)
    chip = me // 2
    my_x, my_z = lax.rem(chip, inner), chip // inner
    sibling = chip * 2 + 1 - core

    def chip_at(dz, dx):
        return lax.rem(my_z + dz + outer, outer) * inner + lax.rem(my_x + dx + inner, inner)

    def dev_at(dz, dx):
        return chip_at(dz, dx) * 2 + core

    sent = []

    def copy(src, dst, sems, index, device):
        return pltpu.make_async_remote_copy(
            src_ref=src,
            dst_ref=dst,
            send_sem=sems.at[(0, *index)],
            recv_sem=sems.at[(1, *index)],
            device_id=device,
            device_id_type=MESH,
        )

    def start(*args):
        one = copy(*args)
        one.start()
        sent.append(one)

    loads = [
        pltpu.make_async_copy(prj, proj.at[:, me], in_sem.at[0]),
        pltpu.make_async_copy(act, xs.at[0], in_sem.at[1]),
        pltpu.make_async_copy(cot, xs.at[pl.ds(1, mats)], in_sem.at[2]),
        pltpu.make_async_copy(mom1, m1, in_sem.at[3]),
        pltpu.make_async_copy(mom2, m2, in_sem.at[4]),
        pltpu.make_async_copy(wts, wbuf, in_sem.at[5]),
    ]
    for one in loads:
        one.start()

    partners = [{"fsdp": sibling}]
    partners += [{"fsdp": dev_at(0, e)} for e in range(1, inner)]
    partners += [{"fsdp": dev_at(d, 0)} for d in range(1, outer)]
    partners += [{"dp": lax.rem(my_dp + s, dp)} for s in range(1, dp)]
    barrier = pltpu.get_barrier_semaphore()
    for partner in partners:
        pl.semaphore_signal(barrier, inc=1, device_id=partner, device_id_type=MESH)
    pl.semaphore_wait(barrier, len(partners))
    loads[0].wait()

    share = shared_rows(rows, dp)
    window = rows - share
    half = window // 2
    window_at = my_dp * share

    def piece(k, owner, h):
        return proj.at[k, owner, pl.ds(pl.multiple_of(window_at + h * half, 16), half)]

    def y_piece(k, owner, plane):
        return proj.at[k, owner, pl.ds(pl.multiple_of(plane * window, 16), share)]

    def z_start(k, h):
        for d in range(1, outer):
            start(piece(k, me, h), piece(k, me, h), gz, (k, h, d - 1), {"fsdp": dev_at(d, 0)})

    def x_start(k, h, d):
        owner = dev_at(-d, 0)
        for e in range(1, inner):
            start(piece(k, owner, h), piece(k, owner, h), gx, (k, h, d, e - 1), {"fsdp": dev_at(0, e)})

    def z_forward(k, h):
        for d in range(1, outer):
            got = piece(k, dev_at(-d, 0), h)
            copy(got, got, gz, (k, h, d - 1), {"fsdp": dev_at(-d, 0)}).wait_recv()
            x_start(k, h, d)

    def y_start(k, d, e):
        if share:
            part = y_piece(k, dev_at(-d, -e), my_dp)
            start(part, part, gy, (k, d, e), {"dp": 1 - my_dp})

    def x_arrived(k, y_too=True):
        for d in range(outer):
            for e in range(1, inner):
                for h in range(2):
                    got = piece(k, dev_at(-d, -e), h)
                    copy(got, got, gx, (k, h, d, e - 1), {"fsdp": dev_at(0, -e)}).wait_recv()
                y_start(k, d, e)

    def to_sibling(k):
        for d in range(outer):
            for e in range(inner):
                owner = dev_at(-d, -e)
                if share and (d or e):
                    got = y_piece(k, owner, 1 - my_dp)
                    copy(got, got, gy, (k, d, e), {"dp": 1 - my_dp}).wait_recv()
                block = proj.at[k, owner]
                start(block, block, gs, (k, d, e), {"fsdp": sibling})

    def from_sibling(k):
        for d in range(outer):
            for e in range(inner):
                block = proj.at[k, chip_at(-d, -e) * 2 + 1 - core]
                copy(block, block, gs, (k, d, e), {"fsdp": sibling}).wait_recv()

    z_start(0, 0)
    x_start(0, 0, 0)
    z_start(0, 1)
    x_start(0, 1, 0)

    loads[1].wait()
    loads[2].wait()

    def columns(f):
        return pl.ds(pl.multiple_of(f * rows, rows), rows)

    def stage(k):
        other = jnp.where(settings[k, 1] == 0, 1 + k, 0)

        def body(c, carry):
            own_t[k, c] = xs[other, :, columns(c * 2 + core)].T
            send_t[k, c] = xs[other, :, columns(c * 2 + 1 - core)].T
            return carry

        lax.fori_loop(0, chips, body, 0)
        start(send_t.at[k], sib_t.at[k], st, (k,), {"fsdp": sibling})

    for k in range(mats):
        stage(k)

    z_forward(0, 0)
    z_start(1, 0)
    x_start(1, 0, 0)
    z_forward(0, 1)
    for d in range(1, outer):
        y_start(0, d, 0)
    z_start(1, 1)
    x_start(1, 1, 0)
    x_arrived(0)
    z_forward(1, 0)
    to_sibling(0)
    z_forward(1, 1)
    for d in range(1, outer):
        y_start(1, d, 0)
    from_sibling(0)

    def coefficients(k):
        projected = jnp.where(settings[k, 1] == 0, 0, 1 + k)
        acc[...] = jnp.zeros_like(acc)

        def body(f, carry):
            acc[...] += jnp.dot(xs[projected, :, columns(f)], proj[k, f], preferred_element_type=F32)
            return carry

        lax.fori_loop(0, fsdp, body, 0)
        own_c[k] = acc[...].astype(BF16)
        start(own_c.at[k], sib_c.at[k], sc, (k,), {"fsdp": sibling})

    def share_arrived(k):
        copy(own_c.at[k], sib_c.at[k], sc, (k,), {"fsdp": sibling}).wait_recv()
        copy(send_t.at[k], sib_t.at[k], st, (k,), {"fsdp": sibling}).wait_recv()

    order = list(range(1, outer)) + [0]

    def partial(k, c):
        return jnp.dot(own_t[k, c], own_c[k], preferred_element_type=F32) + jnp.dot(
            sib_t[k, c], sib_c[k], preferred_element_type=F32
        )

    def reduce_x(k):
        for d in order:
            for e in range(1, inner):
                xsend[k, d, e - 1] = partial(k, chip_at(d, e)).astype(BF16)
                start(xsend.at[k, d, e - 1], xrecv.at[k, d, e - 1], rx, (k, d, e - 1), {"fsdp": dev_at(0, e)})

    def reduce_z(k):
        for d in order:
            total = partial(k, chip_at(d, 0))
            for e in range(1, inner):
                copy(xsend.at[k, d, e - 1], xrecv.at[k, d, e - 1], rx, (k, d, e - 1), {"fsdp": dev_at(0, e)}).wait_recv()
                total += xrecv[k, d, e - 1].astype(F32)
            if d:
                zsend[k, d - 1] = total.astype(BF16)
                start(zsend.at[k, d - 1], zrecv.at[k, d - 1], rz, (k, d - 1), {"fsdp": dev_at(d, 0)})
            else:
                zacc[k] = total

    def reduce_y(k):
        for d in range(1, outer):
            copy(zsend.at[k, d - 1], zrecv.at[k, d - 1], rz, (k, d - 1), {"fsdp": dev_at(d, 0)}).wait_recv()
        total = zacc[k]
        for d in range(1, outer):
            total += zrecv[k, d - 1].astype(F32)
        ybuf[k, my_dp] = total.astype(BF16)
        for s in range(1, dp):
            start(ybuf.at[k, my_dp], ybuf.at[k, my_dp], ry, (k, s - 1), {"dp": lax.rem(my_dp + s, dp)})

    def finish(k):
        for s in range(1, dp):
            got = ybuf.at[k, lax.rem(my_dp - s + dp, dp)]
            copy(got, got, ry, (k, s - 1), {"dp": lax.rem(my_dp + s, dp)}).wait_recv()
        live = lax.broadcasted_iota(jnp.int32, (rows, rank_max), 1) < settings[k, 0]
        total = ybuf[k, 0].astype(F32)
        for s in range(1, dp):
            total += ybuf[k, s].astype(F32)
        grad = total * scale
        first = jnp.where(live, BETA_ONE * m1[k] + (1.0 - BETA_ONE) * grad, 0.0)
        second = jnp.where(live, BETA_TWO * m2[k] + (1.0 - BETA_TWO) * grad * grad, 0.0)
        m1[k] = first
        m2[k] = second
        pltpu.make_async_copy(m1.at[k], m1_out.at[k], out_sem.at[0, k]).start()
        pltpu.make_async_copy(m2.at[k], m2_out.at[k], out_sem.at[1, k]).start()
        nbuf[...] = jnp.where(live, first / (jnp.sqrt(second) + EPSILON), 0.0).astype(BF16)

        def body(f, carry):
            update = lax.dot_general(
                nbuf[...], proj[k, f], (((1,), (1,)), ((), ())), preferred_element_type=F32
            )
            wbuf[k, :, columns(f)] = (wbuf[k, :, columns(f)].astype(F32) - update).astype(BF16)
            return carry

        lax.fori_loop(0, fsdp, body, 0)
        pltpu.make_async_copy(wbuf.at[k], w_out.at[k], out_sem.at[2, k]).start()

    coefficients(0)
    share_arrived(0)
    x_arrived(1)
    reduce_x(0)
    to_sibling(1)
    reduce_z(0)
    from_sibling(1)
    coefficients(1)
    share_arrived(1)
    reduce_x(1)
    reduce_y(0)
    reduce_z(1)
    for one in loads[3:]:
        one.wait()
    finish(0)
    reduce_y(1)
    finish(1)

    for k in range(mats):
        pltpu.make_async_copy(m1.at[k], m1_out.at[k], out_sem.at[0, k]).wait()
        pltpu.make_async_copy(m2.at[k], m2_out.at[k], out_sem.at[1, k]).wait()
        pltpu.make_async_copy(wbuf.at[k], w_out.at[k], out_sem.at[2, k]).wait()
    for one in sent:
        one.wait_send()


def on_device(fsdp, dp, activations, cotangents, weights, projectors, first_moment, second_moment, matrix_settings):
    tokens, features = activations.shape
    mats, rows, rank_max = projectors.shape
    outer, inner = split_axis(fsdp)
    chips = outer * inner
    scale = 1.0 / math.sqrt(tokens * fsdp * dp)
    hbm = pl.BlockSpec(memory_space=pl.ANY)
    sems = pltpu.SemaphoreType.DMA
    flops = 2 * mats * features * rank_max * (2 * tokens + rows) + 2 * mats * tokens * features * rank_max
    return pl.pallas_call(
        functools.partial(kernel, fsdp, dp, scale),
        out_shape=(
            jax.ShapeDtypeStruct(weights.shape, weights.dtype),
            jax.ShapeDtypeStruct(first_moment.shape, first_moment.dtype),
            jax.ShapeDtypeStruct(second_moment.shape, second_moment.dtype),
        ),
        in_specs=[pl.BlockSpec(memory_space=pltpu.SMEM)] + [hbm] * 6,
        out_specs=(hbm, hbm, hbm),
        scratch_shapes=[
            pltpu.VMEM((mats + 1, tokens, features), BF16),
            pltpu.VMEM((mats, fsdp, rows, rank_max), BF16),
            pltpu.VMEM((mats, chips, rows, tokens), BF16),
            pltpu.VMEM((mats, chips, rows, tokens), BF16),
            pltpu.VMEM((mats, chips, rows, tokens), BF16),
            pltpu.VMEM((mats, tokens, rank_max), BF16),
            pltpu.VMEM((mats, tokens, rank_max), BF16),
            pltpu.VMEM((tokens, rank_max), F32),
            pltpu.VMEM((mats, rows, rank_max), F32),
            pltpu.VMEM((mats, outer, inner - 1, rows, rank_max), BF16),
            pltpu.VMEM((mats, outer, inner - 1, rows, rank_max), BF16),
            pltpu.VMEM((mats, outer - 1, rows, rank_max), BF16),
            pltpu.VMEM((mats, outer - 1, rows, rank_max), BF16),
            pltpu.VMEM((mats, dp, rows, rank_max), BF16),
            pltpu.VMEM((mats, rows, features), BF16),
            pltpu.VMEM((mats, rows, rank_max), F32),
            pltpu.VMEM((mats, rows, rank_max), F32),
            pltpu.VMEM((rows, rank_max), BF16),
            sems((6,)),
            sems((3, mats)),
            sems((2, mats, 2, outer - 1)),
            sems((2, mats, 2, outer, inner - 1)),
            sems((2, mats, outer, inner)),
            sems((2, mats, outer, inner)),
            sems((2, mats)),
            sems((2, mats)),
            sems((2, mats, outer, inner - 1)),
            sems((2, mats, outer - 1)),
            sems((2, mats, dp - 1)),
        ],
        compiler_params=pltpu.CompilerParams(
            collective_id=0, has_side_effects=True, vmem_limit_bytes=56 * 1024 * 1024
        ),
        cost_estimate=pl.CostEstimate(flops=flops, bytes_accessed=24 * 1024 * 1024, transcendentals=0),
    )(matrix_settings, activations, cotangents, weights, projectors, first_moment, second_moment)


def solution(mesh):
    return jax.shard_map(
        functools.partial(on_device, mesh.shape["fsdp"], mesh.shape["dp"]),
        mesh=mesh,
        in_specs=(
            P(("fsdp", "dp"), None),
            P(None, ("fsdp", "dp"), None),
            P(None, "fsdp", None),
            P(None, "fsdp", None),
            P(None, "fsdp", None),
            P(None, "fsdp", None),
            P(),
        ),
        out_specs=(P(None, "fsdp", None), P(None, "fsdp", None), P(None, "fsdp", None)),
        check_vma=False,
    )
```

```python
import functools
import math

import jax
import jax.numpy as jnp
from jax import lax
from jax.experimental import pallas as pl
from jax.experimental.pallas import tpu as pltpu
from jax.sharding import PartitionSpec as P

BETA_ONE = 0.9
BETA_TWO = 0.95
EPSILON = 1e-08
MESH = pl.DeviceIdType.MESH
BF16, F32 = jnp.bfloat16, jnp.float32


def split_axis(fsdp):
    chips = fsdp // 2
    inner = 1
    while (2 * inner) ** 2 <= chips and chips % (2 * inner) == 0:
        inner *= 2
    return chips // inner, inner


def shared_rows(rows, dp):
    return (rows * 3 // 8) // 32 * 32 if dp == 2 else 0


def zone_rows(rows, dp):
    return (rows // 4) // 16 * 16 if dp == 2 else 0


def kernel(
    fsdp, dp, scale, cols,
    settings, act, cot, wts, prj, mom1, mom2, w_out, m1_out, m2_out,
    xs, proj, own_t, sib_t, send_t, own_c, sib_c, cacc, acc, zacc, yfirst, yrecv, xsend, xrecv, zsend, zrecv, ybuf, wbuf, m1, m2, nbuf,
    in_sem, out_sem, gz, gx, gy, gs, st, sc, ry0, rx, rz, ry,
):
    mats, _, rows, rank_max = proj.shape
    tokens = act.shape[0]
    outer, inner = split_axis(fsdp)
    chips = outer * inner
    me, my_dp = lax.axis_index("fsdp"), lax.axis_index("dp")
    core = lax.rem(me, 2)
    chip = me // 2
    my_x, my_z = lax.rem(chip, inner), chip // inner
    sibling = chip * 2 + 1 - core

    def chip_at(dz, dx):
        return lax.rem(my_z + dz + outer, outer) * inner + lax.rem(my_x + dx + inner, inner)

    def dev_at(dz, dx):
        return chip_at(dz, dx) * 2 + core

    sent = []

    def copy(src, dst, sems, index, device):
        return pltpu.make_async_remote_copy(
            src_ref=src,
            dst_ref=dst,
            send_sem=sems.at[(0, *index)],
            recv_sem=sems.at[(1, *index)],
            device_id=device,
            device_id_type=MESH,
        )

    def start(*args):
        one = copy(*args)
        one.start()
        sent.append(one)

    loads = [
        pltpu.make_async_copy(prj, proj.at[:, me], in_sem.at[0]),
        pltpu.make_async_copy(act, xs.at[0], in_sem.at[1]),
        pltpu.make_async_copy(cot, xs.at[pl.ds(1, mats)], in_sem.at[2]),
        pltpu.make_async_copy(mom1, m1, in_sem.at[3]),
        pltpu.make_async_copy(mom2, m2, in_sem.at[4]),
        pltpu.make_async_copy(wts, wbuf, in_sem.at[5]),
    ]
    for one in loads:
        one.start()

    partners = [{"fsdp": sibling}]
    partners += [{"fsdp": dev_at(0, e)} for e in range(1, inner)]
    partners += [{"fsdp": dev_at(d, 0)} for d in range(1, outer)]
    partners += [{"dp": lax.rem(my_dp + s, dp)} for s in range(1, dp)]
    barrier = pltpu.get_barrier_semaphore()
    for partner in partners:
        pl.semaphore_signal(barrier, inc=1, device_id=partner, device_id_type=MESH)
    pl.semaphore_wait(barrier, len(partners))
    loads[0].wait()

    share = shared_rows(rows, dp)
    window = rows - share
    half = window // 2
    window_at = my_dp * share

    def piece(k, owner, h):
        return proj.at[k, owner, pl.ds(pl.multiple_of(window_at + h * half, 16), half), pl.ds(0, cols[k])]

    def y_piece(k, owner, plane):
        return proj.at[k, owner, pl.ds(pl.multiple_of(plane * window, 16), share), pl.ds(0, cols[k])]

    def z_start(k, h):
        for d in range(1, outer):
            start(piece(k, me, h), piece(k, me, h), gz, (k, h, d - 1), {"fsdp": dev_at(d, 0)})

    def x_start(k, h, d):
        owner = dev_at(-d, 0)
        for e in range(1, inner):
            start(piece(k, owner, h), piece(k, owner, h), gx, (k, h, d, e - 1), {"fsdp": dev_at(0, e)})

    def z_forward(k, h):
        for d in range(1, outer):
            got = piece(k, dev_at(-d, 0), h)
            copy(got, got, gz, (k, h, d - 1), {"fsdp": dev_at(-d, 0)}).wait_recv()
            x_start(k, h, d)

    def y_start(k, d, e):
        if share:
            part = y_piece(k, dev_at(-d, -e), my_dp)
            start(part, part, gy, (k, d, e), {"dp": 1 - my_dp})

    def x_arrived(k, d):
        for e in range(1, inner):
            for h in range(2):
                got = piece(k, dev_at(-d, -e), h)
                copy(got, got, gx, (k, h, d, e - 1), {"fsdp": dev_at(0, -e)}).wait_recv()
            y_start(k, d, e)

    blocks = [(d, e) for e in range(inner) for d in range(outer)]

    def to_sibling(k, d, e):
        owner = dev_at(-d, -e)
        if share and (d or e):
            got = y_piece(k, owner, 1 - my_dp)
            copy(got, got, gy, (k, d, e), {"dp": 1 - my_dp}).wait_recv()
        block = proj.at[k, owner, :, pl.ds(0, cols[k])]
        start(block, block, gs, (k, d, e), {"fsdp": sibling})
        accumulate(k, owner)

    def from_sibling(k, d, e):
        owner = chip_at(-d, -e) * 2 + 1 - core
        block = proj.at[k, owner, :, pl.ds(0, cols[k])]
        copy(block, block, gs, (k, d, e), {"fsdp": sibling}).wait_recv()
        accumulate(k, owner)

    def gather(k):
        for i, at in enumerate(blocks):
            to_sibling(k, *at)
            if i:
                from_sibling(k, *blocks[i - 1])
        from_sibling(k, *blocks[-1])

    def columns(f):
        return pl.ds(pl.multiple_of(f * rows, rows), rows)

    def accumulate(k, owner):
        projected = jnp.where(settings[k, 1] == 0, 0, 1 + k)
        w = cols[k]
        cacc[k, :, :w] += jnp.dot(
            xs[projected, :, columns(owner)], proj[k, owner, :, :w], preferred_element_type=F32
        )

    z_start(0, 0)
    x_start(0, 0, 0)
    z_start(0, 1)
    x_start(0, 1, 0)

    loads[1].wait()
    loads[2].wait()

    def stage(k):
        other = jnp.where(settings[k, 1] == 0, 1 + k, 0)

        def body(c, carry):
            own_t[k, c] = xs[other, :, columns(c * 2 + core)].T
            send_t[k, c] = xs[other, :, columns(c * 2 + 1 - core)].T
            return carry

        lax.fori_loop(0, chips, body, 0)
        start(send_t.at[k], sib_t.at[k], st, (k,), {"fsdp": sibling})

    for k in range(mats):
        stage(k)
        cacc[k] = jnp.zeros((tokens, rank_max), F32)
        if k == 0:
            x_arrived(0, 0)

    z_forward(0, 0)
    z_start(1, 0)
    x_start(1, 0, 0)
    z_forward(0, 1)
    for d in range(1, outer):
        y_start(0, d, 0)
    z_start(1, 1)
    x_start(1, 1, 0)
    for d in range(1, outer):
        x_arrived(0, d)
    z_forward(1, 0)
    x_arrived(1, 0)
    for i in range(outer):
        to_sibling(0, *blocks[i])
    for i in range(outer):
        from_sibling(0, *blocks[i])
    z_forward(1, 1)
    for d in range(1, outer):
        y_start(1, d, 0)
    for i in range(outer, len(blocks)):
        to_sibling(0, *blocks[i])
        if i > outer:
            from_sibling(0, *blocks[i - 1])
    from_sibling(0, *blocks[-1])

    def coefficient_copy(k):
        part = pl.ds(0, cols[k])
        return own_c.at[k, :, part], sib_c.at[k, :, part], sc, (k,), {"fsdp": sibling}

    def coefficients(k):
        w = cols[k]
        own_c[k, :, :w] = cacc[k, :, :w].astype(BF16)
        start(*coefficient_copy(k))

    def share_arrived(k):
        copy(*coefficient_copy(k)).wait_recv()
        copy(send_t.at[k], sib_t.at[k], st, (k,), {"fsdp": sibling}).wait_recv()

    order = list(range(1, outer)) + [0]
    zone = zone_rows(rows, dp)
    span = rows - zone
    span_at = my_dp * zone
    zone_in_span = my_dp * (span - zone)

    def partial(k, c, at, size):
        part = pl.ds(pl.multiple_of(at, 16), size)
        w = cols[k]
        return jnp.dot(own_t[k, c, part], own_c[k, :, :w], preferred_element_type=F32) + jnp.dot(
            sib_t[k, c, part], sib_c[k, :, :w], preferred_element_type=F32
        )

    def zsum(k, d, e):
        ref = (yfirst.at[k, d, e, :, pl.ds(0, cols[k])], yrecv.at[k, d, e, :, pl.ds(0, cols[k])])
        return (*ref, ry0, (k, d, e), {"dp": 1 - my_dp})

    def reduce_first(k, e):
        if zone:
            for d in order:
                mine = partial(k, chip_at(d, e), (1 - my_dp) * span, zone)
                yfirst[k, d, e, :, : cols[k]] = mine.astype(BF16)
                start(*zsum(k, d, e))

    def spanned(k, d, e):
        w = cols[k]
        acc[:span, :w] = partial(k, chip_at(d, e), span_at, span)
        if zone:
            copy(*zsum(k, d, e)).wait_recv()
            acc[pl.ds(pl.multiple_of(zone_in_span, 16), zone), :w] += yrecv[k, d, e, :, :w].astype(F32)
        return acc[:span, :w]

    def x_sum(k, d, e):
        part = pl.ds(0, cols[k])
        return (
            xsend.at[k, d, e - 1, :, part], xrecv.at[k, d, e - 1, :, part], rx, (k, d, e - 1), {"fsdp": dev_at(0, e)}
        )

    def z_sum(k, d):
        part = pl.ds(0, cols[k])
        return zsend.at[k, d - 1, :, part], zrecv.at[k, d - 1, :, part], rz, (k, d - 1), {"fsdp": dev_at(d, 0)}

    def y_sum(k, s, plane):
        got = ybuf.at[k, plane, :, pl.ds(0, cols[k])]
        return got, got, ry, (k, s - 1), {"dp": lax.rem(my_dp + s, dp)}

    def reduce_x(k):
        for d in order:
            for e in range(1, inner):
                xsend[k, d, e - 1, :, : cols[k]] = spanned(k, d, e).astype(BF16)
                start(*x_sum(k, d, e))

    def reduce_z(k, d):
        w = cols[k]
        total = spanned(k, d, 0)
        for e in range(1, inner):
            copy(*x_sum(k, d, e)).wait_recv()
            total += xrecv[k, d, e - 1, :, :w].astype(F32)
        if d:
            zsend[k, d - 1, :, :w] = total.astype(BF16)
            start(*z_sum(k, d))
        else:
            zacc[k, :, :w] = total

    def reduce_y(k):
        w = cols[k]
        for d in range(1, outer):
            copy(*z_sum(k, d)).wait_recv()
        total = zacc[k, :, :w]
        for d in range(1, outer):
            total += zrecv[k, d - 1, :, :w].astype(F32)
        ybuf[k, my_dp, :, :w] = total.astype(BF16)
        for s in range(1, dp):
            start(*y_sum(k, s, my_dp))

    def finish_rows(k, at, size, terms):
        w = cols[k]
        here = pl.ds(at, size)
        total = None
        for plane, first_row in terms:
            term = ybuf[k, plane, first_row : first_row + size, :w].astype(F32)
            total = term if total is None else total + term
        live = lax.broadcasted_iota(jnp.int32, (size, w), 1) < settings[k, 0]
        grad = total * scale
        first = jnp.where(live, BETA_ONE * m1[k, here, :w] + (1.0 - BETA_ONE) * grad, 0.0)
        second = jnp.where(live, BETA_TWO * m2[k, here, :w] + (1.0 - BETA_TWO) * grad * grad, 0.0)
        m1[k, here, :w] = first
        m2[k, here, :w] = second
        nbuf[here, :w] = jnp.where(live, first / (jnp.sqrt(second) + EPSILON), 0.0).astype(BF16)

    def finish(k):
        w = cols[k]
        for s in range(1, dp):
            copy(*y_sum(k, s, lax.rem(my_dp - s + dp, dp))).wait_recv()
        if zone:
            finish_rows(k, 0, zone, [(0, 0)])
            finish_rows(k, zone, span - zone, [(0, zone), (1, 0)])
            finish_rows(k, span, zone, [(1, span - zone)])
        else:
            finish_rows(k, 0, rows, [(plane, 0) for plane in range(dp)])
        if w < rank_max:
            m1[k, :, w:] = jnp.zeros((rows, rank_max - w), F32)
            m2[k, :, w:] = jnp.zeros((rows, rank_max - w), F32)
        pltpu.make_async_copy(m1.at[k], m1_out.at[k], out_sem.at[0, k]).start()
        pltpu.make_async_copy(m2.at[k], m2_out.at[k], out_sem.at[1, k]).start()

        def body(f, carry):
            update = lax.dot_general(
                nbuf[:, :w], proj[k, f, :, :w], (((1,), (1,)), ((), ())), preferred_element_type=F32
            )
            wbuf[k, :, columns(f)] = (wbuf[k, :, columns(f)].astype(F32) - update).astype(BF16)
            return carry

        lax.fori_loop(0, fsdp, body, 0)
        pltpu.make_async_copy(wbuf.at[k], w_out.at[k], out_sem.at[2, k]).start()

    coefficients(0)
    for d in range(1, outer):
        x_arrived(1, d)
    share_arrived(0)
    for e in range(1, inner):
        reduce_first(0, e)
    reduce_x(0)
    reduce_first(0, 0)
    reduce_z(0, order[0])
    gather(1)
    coefficients(1)
    share_arrived(1)
    for e in range(1, inner):
        reduce_first(1, e)
    reduce_x(1)
    reduce_first(1, 0)
    for d in order[1:]:
        reduce_z(0, d)
    reduce_y(0)
    for d in order[:2]:
        reduce_z(1, d)
    for one in loads[3:]:
        one.wait()
    finish(0)
    for d in order[2:]:
        reduce_z(1, d)
    reduce_y(1)
    finish(1)

    for k in range(mats):
        pltpu.make_async_copy(m1.at[k], m1_out.at[k], out_sem.at[0, k]).wait()
        pltpu.make_async_copy(m2.at[k], m2_out.at[k], out_sem.at[1, k]).wait()
        pltpu.make_async_copy(wbuf.at[k], w_out.at[k], out_sem.at[2, k]).wait()
    for one in sent:
        one.wait_send()


def step(fsdp, dp, cols, number, activations, cotangents, weights, projectors, first_moment, second_moment, matrix_settings):
    tokens, features = activations.shape
    mats, rows, rank_max = projectors.shape
    outer, inner = split_axis(fsdp)
    chips = outer * inner
    zone = zone_rows(rows, dp)
    span = rows - zone
    scale = 1.0 / math.sqrt(tokens * fsdp * dp)
    hbm = pl.BlockSpec(memory_space=pl.ANY)
    sems = pltpu.SemaphoreType.DMA
    flops = 2 * mats * features * rank_max * (2 * tokens + rows) + 2 * mats * tokens * features * rank_max
    return pl.pallas_call(
        functools.partial(kernel, fsdp, dp, scale, cols),
        out_shape=(
            jax.ShapeDtypeStruct(weights.shape, weights.dtype),
            jax.ShapeDtypeStruct(first_moment.shape, first_moment.dtype),
            jax.ShapeDtypeStruct(second_moment.shape, second_moment.dtype),
        ),
        in_specs=[pl.BlockSpec(memory_space=pltpu.SMEM)] + [hbm] * 6,
        out_specs=(hbm, hbm, hbm),
        scratch_shapes=[
            pltpu.VMEM((mats + 1, tokens, features), BF16),
            pltpu.VMEM((mats, fsdp, rows, rank_max), BF16),
            pltpu.VMEM((mats, chips, rows, tokens), BF16),
            pltpu.VMEM((mats, chips, rows, tokens), BF16),
            pltpu.VMEM((mats, chips, rows, tokens), BF16),
            pltpu.VMEM((mats, tokens, rank_max), BF16),
            pltpu.VMEM((mats, tokens, rank_max), BF16),
            pltpu.VMEM((mats, tokens, rank_max), F32),
            pltpu.VMEM((rows, rank_max), F32),
            pltpu.VMEM((mats, span, rank_max), F32),
            pltpu.VMEM((mats, outer, inner, max(zone, 16), rank_max), BF16),
            pltpu.VMEM((mats, outer, inner, max(zone, 16), rank_max), BF16),
            pltpu.VMEM((mats, outer, inner - 1, span, rank_max), BF16),
            pltpu.VMEM((mats, outer, inner - 1, span, rank_max), BF16),
            pltpu.VMEM((mats, outer - 1, span, rank_max), BF16),
            pltpu.VMEM((mats, outer - 1, span, rank_max), BF16),
            pltpu.VMEM((mats, dp, span, rank_max), BF16),
            pltpu.VMEM((mats, rows, features), BF16),
            pltpu.VMEM((mats, rows, rank_max), F32),
            pltpu.VMEM((mats, rows, rank_max), F32),
            pltpu.VMEM((rows, rank_max), BF16),
            sems((6,)),
            sems((3, mats)),
            sems((2, mats, 2, outer - 1)),
            sems((2, mats, 2, outer, inner - 1)),
            sems((2, mats, outer, inner)),
            sems((2, mats, outer, inner)),
            sems((2, mats)),
            sems((2, mats)),
            sems((2, mats, outer, inner)),
            sems((2, mats, outer, inner - 1)),
            sems((2, mats, outer - 1)),
            sems((2, mats, dp - 1)),
        ],
        compiler_params=pltpu.CompilerParams(
            collective_id=number, has_side_effects=True, vmem_limit_bytes=56 * 1024 * 1024
        ),
        cost_estimate=pl.CostEstimate(flops=flops, bytes_accessed=24 * 1024 * 1024, transcendentals=0),
    )(matrix_settings, activations, cotangents, weights, projectors, first_moment, second_moment)


def on_device(fsdp, dp, *args):
    rank_max, settings = args[3].shape[2], args[-1]
    mats = settings.shape[0]
    widths = [w for w in range(256, rank_max, 128)] + [rank_max]
    if mats != 2 or len(widths) == 1:
        return step(fsdp, dp, (rank_max,) * mats, 0, *args)
    pairs = [(rank_max, w) for w in widths] + [(w, rank_max) for w in widths[:-1]]
    last = len(widths) - 1
    at = jnp.clip((settings[:, 0] + 127) // 128 - 2, 0, last)
    chosen = jnp.where(at[0] == last, at[1], last + 1 + at[0])
    return lax.switch(
        chosen, [functools.partial(step, fsdp, dp, pair, i) for i, pair in enumerate(pairs)], *args
    )


def solution(mesh):
    return jax.shard_map(
        functools.partial(on_device, mesh.shape["fsdp"], mesh.shape["dp"]),
        mesh=mesh,
        in_specs=(
            P(("fsdp", "dp"), None),
            P(None, ("fsdp", "dp"), None),
            P(None, "fsdp", None),
            P(None, "fsdp", None),
            P(None, "fsdp", None),
            P(None, "fsdp", None),
            P(),
        ),
        out_specs=(P(None, "fsdp", None), P(None, "fsdp", None), P(None, "fsdp", None)),
        check_vma=False,
    )
```

```python
import functools
import math

import jax
import jax.numpy as jnp
from jax import lax
from jax.experimental import pallas as pl
from jax.experimental.pallas import tpu as pltpu
from jax.sharding import PartitionSpec as P

BETA_ONE = 0.9
BETA_TWO = 0.95
EPSILON = 1e-08
MESH = pl.DeviceIdType.MESH
BF16, F32 = jnp.bfloat16, jnp.float32


def split_axis(fsdp):
    chips = fsdp // 2
    inner = 1
    while (2 * inner) ** 2 <= chips and chips % (2 * inner) == 0:
        inner *= 2
    return chips // inner, inner


def shared_rows(rows, dp):
    return (rows * 3 // 8) // 32 * 32 if dp == 2 else 0


def zone_of(width, dp):
    return (width // 4) // 16 * 16 if dp == 2 else 0


def kernel(
    fsdp, dp, scale, cols,
    settings, act, cot, wts, prj, mom1, mom2, w_out, m1_out, m2_out,
    xs, proj, sib_x, own_c, sib_c, cacc, acc, zacc, yfirst, yrecv, xsend, xrecv, zsend, zrecv, ybuf, wbuf, m1, m2, nbuf,
    in_sem, out_sem, gz, gx, gy, gs, st, sc, ry0, rx, rz, ry,
):
    mats, _, rows, rank_max = proj.shape
    tokens = act.shape[0]
    outer, inner = split_axis(fsdp)
    chips = outer * inner
    me, my_dp = lax.axis_index("fsdp"), lax.axis_index("dp")
    core = lax.rem(me, 2)
    chip = me // 2
    my_x, my_z = lax.rem(chip, inner), chip // inner
    sibling = chip * 2 + 1 - core

    def chip_at(dz, dx):
        return lax.rem(my_z + dz + outer, outer) * inner + lax.rem(my_x + dx + inner, inner)

    def dev_at(dz, dx):
        return chip_at(dz, dx) * 2 + core

    sent = []

    def copy(src, dst, sems, index, device):
        return pltpu.make_async_remote_copy(
            src_ref=src,
            dst_ref=dst,
            send_sem=sems.at[(0, *index)],
            recv_sem=sems.at[(1, *index)],
            device_id=device,
            device_id_type=MESH,
        )

    def start(*args):
        one = copy(*args)
        one.start()
        sent.append(one)

    loads = [
        pltpu.make_async_copy(prj, proj.at[:, me], in_sem.at[0]),
        pltpu.make_async_copy(act, xs.at[0], in_sem.at[1]),
        pltpu.make_async_copy(cot, xs.at[pl.ds(1, mats)], in_sem.at[2]),
        pltpu.make_async_copy(mom1, m1, in_sem.at[3]),
        pltpu.make_async_copy(mom2, m2, in_sem.at[4]),
        pltpu.make_async_copy(wts, wbuf, in_sem.at[5]),
    ]
    for one in loads:
        one.start()

    partners = [{"fsdp": sibling}]
    partners += [{"fsdp": dev_at(0, e)} for e in range(1, inner)]
    partners += [{"fsdp": dev_at(d, 0)} for d in range(1, outer)]
    partners += [{"dp": lax.rem(my_dp + s, dp)} for s in range(1, dp)]
    barrier = pltpu.get_barrier_semaphore()
    for partner in partners:
        pl.semaphore_signal(barrier, inc=1, device_id=partner, device_id_type=MESH)
    pl.semaphore_wait(barrier, len(partners))
    loads[0].wait()

    share = shared_rows(rows, dp)
    window = rows - share
    half = window // 2
    window_at = my_dp * share

    def piece(k, owner, h):
        return proj.at[k, owner, pl.ds(pl.multiple_of(window_at + h * half, 16), half), pl.ds(0, cols[k])]

    def y_piece(k, owner, plane):
        return proj.at[k, owner, pl.ds(pl.multiple_of(plane * window, 16), share), pl.ds(0, cols[k])]

    def z_start(k, h):
        for d in range(1, outer):
            start(piece(k, me, h), piece(k, me, h), gz, (k, h, d - 1), {"fsdp": dev_at(d, 0)})

    def x_start(k, h, d):
        owner = dev_at(-d, 0)
        for e in range(1, inner):
            start(piece(k, owner, h), piece(k, owner, h), gx, (k, h, d, e - 1), {"fsdp": dev_at(0, e)})

    def z_forward(k, h):
        for d in range(1, outer):
            got = piece(k, dev_at(-d, 0), h)
            copy(got, got, gz, (k, h, d - 1), {"fsdp": dev_at(-d, 0)}).wait_recv()
            x_start(k, h, d)

    def y_start(k, d, e):
        if share:
            part = y_piece(k, dev_at(-d, -e), my_dp)
            start(part, part, gy, (k, d, e), {"dp": 1 - my_dp})

    def x_arrived(k, d):
        for e in range(1, inner):
            for h in range(2):
                got = piece(k, dev_at(-d, -e), h)
                copy(got, got, gx, (k, h, d, e - 1), {"fsdp": dev_at(0, -e)}).wait_recv()
            y_start(k, d, e)

    blocks = [(d, e) for e in range(inner) for d in range(outer)]

    def to_sibling(k, d, e):
        owner = dev_at(-d, -e)
        if share and (d or e):
            got = y_piece(k, owner, 1 - my_dp)
            copy(got, got, gy, (k, d, e), {"dp": 1 - my_dp}).wait_recv()
        block = proj.at[k, owner, :, pl.ds(0, cols[k])]
        start(block, block, gs, (k, d, e), {"fsdp": sibling})
        accumulate(k, owner)

    def from_sibling(k, d, e):
        owner = chip_at(-d, -e) * 2 + 1 - core
        block = proj.at[k, owner, :, pl.ds(0, cols[k])]
        copy(block, block, gs, (k, d, e), {"fsdp": sibling}).wait_recv()
        accumulate(k, owner)

    def gather(k):
        for i, at in enumerate(blocks):
            to_sibling(k, *at)
            if i:
                from_sibling(k, *blocks[i - 1])
        from_sibling(k, *blocks[-1])

    def columns(f):
        return pl.ds(pl.multiple_of(f * rows, rows), rows)

    def accumulate(k, owner):
        projected = jnp.where(settings[k, 1] == 0, 0, 1 + k)
        w = cols[k]
        cacc[k, :, :w] += jnp.dot(
            xs[projected, :, columns(owner)], proj[k, owner, :, :w], preferred_element_type=F32
        )

    z_start(0, 0)
    x_start(0, 0, 0)
    z_start(0, 1)
    x_start(0, 1, 0)

    loads[1].wait()
    loads[2].wait()

    def operand_copy(c):
        return xs.at[:, :, columns(c * 2 + 1 - core)], sib_x.at[:, c], st, (c,), {"fsdp": sibling}

    for c in range(chips):
        start(*operand_copy(c))

    for k in range(mats):
        cacc[k] = jnp.zeros((tokens, rank_max), F32)
        if k == 0:
            x_arrived(0, 0)

    z_forward(0, 0)
    z_start(1, 0)
    x_start(1, 0, 0)
    z_forward(0, 1)
    for d in range(1, outer):
        y_start(0, d, 0)
    z_start(1, 1)
    x_start(1, 1, 0)
    for d in range(1, outer):
        x_arrived(0, d)
    z_forward(1, 0)
    x_arrived(1, 0)
    for i in range(outer):
        to_sibling(0, *blocks[i])
    for i in range(outer):
        from_sibling(0, *blocks[i])
    z_forward(1, 1)
    for d in range(1, outer):
        y_start(1, d, 0)
    for i in range(outer, len(blocks)):
        to_sibling(0, *blocks[i])
        if i > outer:
            from_sibling(0, *blocks[i - 1])
    from_sibling(0, *blocks[-1])

    def coefficient_copy(k):
        part = pl.ds(0, cols[k])
        return own_c.at[k, part], sib_c.at[k, part], sc, (k,), {"fsdp": sibling}

    def coefficients(k):
        w = cols[k]
        own_c[k, :w] = cacc[k, :, :w].astype(BF16).T
        start(*coefficient_copy(k))

    def share_arrived(k):
        copy(*coefficient_copy(k)).wait_recv()
        if k == 0:
            for c in range(chips):
                copy(*operand_copy(c)).wait_recv()

    order = list(range(1, outer)) + [0]
    zones = [zone_of(w, dp) for w in cols]
    spans = [w - z for w, z in zip(cols, zones)]

    def partial(k, c, at, size):
        other = jnp.where(settings[k, 1] == 0, 1 + k, 0)
        part = pl.ds(pl.multiple_of(at, 16), size)
        return jnp.dot(
            own_c[k, part], xs[other, :, columns(c * 2 + core)], preferred_element_type=F32
        ) + jnp.dot(sib_c[k, part], sib_x[other, c], preferred_element_type=F32)

    def zsum(k, d, e):
        part = pl.ds(0, zones[k])
        return yfirst.at[k, d, e, part], yrecv.at[k, d, e, part], ry0, (k, d, e), {"dp": 1 - my_dp}

    def reduce_first(k, e):
        if zones[k]:
            for d in order:
                mine = partial(k, chip_at(d, e), (1 - my_dp) * spans[k], zones[k])
                yfirst[k, d, e, : zones[k]] = mine.astype(BF16)
                start(*zsum(k, d, e))

    def spanned(k, d, e):
        zone, span = zones[k], spans[k]
        acc[:span] = partial(k, chip_at(d, e), my_dp * zone, span)
        if zone:
            copy(*zsum(k, d, e)).wait_recv()
            acc[pl.ds(pl.multiple_of(my_dp * (span - zone), 16), zone)] += yrecv[k, d, e, :zone].astype(F32)
        return acc[:span]

    def x_sum(k, d, e):
        part = pl.ds(0, spans[k])
        return (
            xsend.at[k, d, e - 1, part], xrecv.at[k, d, e - 1, part], rx, (k, d, e - 1), {"fsdp": dev_at(0, e)}
        )

    def z_sum(k, d):
        part = pl.ds(0, spans[k])
        return zsend.at[k, d - 1, part], zrecv.at[k, d - 1, part], rz, (k, d - 1), {"fsdp": dev_at(d, 0)}

    def y_sum(k, s, plane):
        got = ybuf.at[k, plane, pl.ds(0, spans[k])]
        return got, got, ry, (k, s - 1), {"dp": lax.rem(my_dp + s, dp)}

    def reduce_x(k):
        for d in order:
            for e in range(1, inner):
                xsend[k, d, e - 1, : spans[k]] = spanned(k, d, e).astype(BF16)
                start(*x_sum(k, d, e))

    def reduce_z(k, d):
        w = spans[k]
        total = spanned(k, d, 0)
        for e in range(1, inner):
            copy(*x_sum(k, d, e)).wait_recv()
            total += xrecv[k, d, e - 1, :w].astype(F32)
        if d:
            zsend[k, d - 1, :w] = total.astype(BF16)
            start(*z_sum(k, d))
        else:
            zacc[k, :w] = total

    def reduce_y(k):
        w = spans[k]
        for d in range(1, outer):
            copy(*z_sum(k, d)).wait_recv()
        total = zacc[k, :w]
        for d in range(1, outer):
            total += zrecv[k, d - 1, :w].astype(F32)
        ybuf[k, my_dp, :w] = total.astype(BF16)
        for s in range(1, dp):
            start(*y_sum(k, s, my_dp))

    def finish(k):
        w, zone, span = cols[k], zones[k], spans[k]
        for s in range(1, dp):
            copy(*y_sum(k, s, lax.rem(my_dp - s + dp, dp))).wait_recv()
        common = ybuf[k, 0, zone:span].astype(F32)
        for plane in range(1, dp):
            common += ybuf[k, plane, : span - zone].astype(F32)
        acc[zone:span] = common
        if zone:
            acc[:zone] = ybuf[k, 0, :zone].astype(F32)
            acc[span:w] = ybuf[k, 1, span - zone : span].astype(F32)
        grad = acc[:w].T * scale
        live = lax.broadcasted_iota(jnp.int32, (rows, w), 1) < settings[k, 0]
        first = jnp.where(live, BETA_ONE * m1[k, :, :w] + (1.0 - BETA_ONE) * grad, 0.0)
        second = jnp.where(live, BETA_TWO * m2[k, :, :w] + (1.0 - BETA_TWO) * grad * grad, 0.0)
        m1[k, :, :w] = first
        m2[k, :, :w] = second
        nbuf[:, :w] = jnp.where(live, first / (jnp.sqrt(second) + EPSILON), 0.0).astype(BF16)
        if w < rank_max:
            m1[k, :, w:] = jnp.zeros((rows, rank_max - w), F32)
            m2[k, :, w:] = jnp.zeros((rows, rank_max - w), F32)
        pltpu.make_async_copy(m1.at[k], m1_out.at[k], out_sem.at[0, k]).start()
        pltpu.make_async_copy(m2.at[k], m2_out.at[k], out_sem.at[1, k]).start()

        def body(f, carry):
            update = lax.dot_general(
                nbuf[:, :w], proj[k, f, :, :w], (((1,), (1,)), ((), ())), preferred_element_type=F32
            )
            wbuf[k, :, columns(f)] = (wbuf[k, :, columns(f)].astype(F32) - update).astype(BF16)
            return carry

        lax.fori_loop(0, fsdp, body, 0)
        pltpu.make_async_copy(wbuf.at[k], w_out.at[k], out_sem.at[2, k]).start()

    coefficients(0)
    for d in range(1, outer):
        x_arrived(1, d)
    share_arrived(0)
    for e in range(1, inner):
        reduce_first(0, e)
    reduce_x(0)
    reduce_first(0, 0)
    reduce_z(0, order[0])
    gather(1)
    coefficients(1)
    share_arrived(1)
    for e in range(1, inner):
        reduce_first(1, e)
    reduce_x(1)
    reduce_first(1, 0)
    for d in order[1:]:
        reduce_z(0, d)
    reduce_y(0)
    for d in order[:2]:
        reduce_z(1, d)
    for one in loads[3:]:
        one.wait()
    finish(0)
    for d in order[2:]:
        reduce_z(1, d)
    reduce_y(1)
    finish(1)

    for k in range(mats):
        pltpu.make_async_copy(m1.at[k], m1_out.at[k], out_sem.at[0, k]).wait()
        pltpu.make_async_copy(m2.at[k], m2_out.at[k], out_sem.at[1, k]).wait()
        pltpu.make_async_copy(wbuf.at[k], w_out.at[k], out_sem.at[2, k]).wait()
    for one in sent:
        one.wait_send()


def step(fsdp, dp, cols, number, activations, cotangents, weights, projectors, first_moment, second_moment, matrix_settings):
    tokens, features = activations.shape
    mats, rows, rank_max = projectors.shape
    outer, inner = split_axis(fsdp)
    chips = outer * inner
    zone = zone_of(rank_max, dp)
    span = rank_max - zone
    scale = 1.0 / math.sqrt(tokens * fsdp * dp)
    hbm = pl.BlockSpec(memory_space=pl.ANY)
    sems = pltpu.SemaphoreType.DMA
    flops = 2 * mats * features * rank_max * (2 * tokens + rows) + 2 * mats * tokens * features * rank_max
    return pl.pallas_call(
        functools.partial(kernel, fsdp, dp, scale, cols),
        out_shape=(
            jax.ShapeDtypeStruct(weights.shape, weights.dtype),
            jax.ShapeDtypeStruct(first_moment.shape, first_moment.dtype),
            jax.ShapeDtypeStruct(second_moment.shape, second_moment.dtype),
        ),
        in_specs=[pl.BlockSpec(memory_space=pltpu.SMEM)] + [hbm] * 6,
        out_specs=(hbm, hbm, hbm),
        scratch_shapes=[
            pltpu.VMEM((mats + 1, tokens, features), BF16),
            pltpu.VMEM((mats, fsdp, rows, rank_max), BF16),
            pltpu.VMEM((mats + 1, chips, tokens, rows), BF16),
            pltpu.VMEM((mats, rank_max, tokens), BF16),
            pltpu.VMEM((mats, rank_max, tokens), BF16),
            pltpu.VMEM((mats, tokens, rank_max), F32),
            pltpu.VMEM((rank_max, rows), F32),
            pltpu.VMEM((mats, span, rows), F32),
            pltpu.VMEM((mats, outer, inner, max(zone, 16), rows), BF16),
            pltpu.VMEM((mats, outer, inner, max(zone, 16), rows), BF16),
            pltpu.VMEM((mats, outer, inner - 1, span, rows), BF16),
            pltpu.VMEM((mats, outer, inner - 1, span, rows), BF16),
            pltpu.VMEM((mats, outer - 1, span, rows), BF16),
            pltpu.VMEM((mats, outer - 1, span, rows), BF16),
            pltpu.VMEM((mats, dp, span, rows), BF16),
            pltpu.VMEM((mats, rows, features), BF16),
            pltpu.VMEM((mats, rows, rank_max), F32),
            pltpu.VMEM((mats, rows, rank_max), F32),
            pltpu.VMEM((rows, rank_max), BF16),
            sems((6,)),
            sems((3, mats)),
            sems((2, mats, 2, outer - 1)),
            sems((2, mats, 2, outer, inner - 1)),
            sems((2, mats, outer, inner)),
            sems((2, mats, outer, inner)),
            sems((2, chips)),
            sems((2, mats)),
            sems((2, mats, outer, inner)),
            sems((2, mats, outer, inner - 1)),
            sems((2, mats, outer - 1)),
            sems((2, mats, dp - 1)),
        ],
        compiler_params=pltpu.CompilerParams(
            collective_id=number, has_side_effects=True, vmem_limit_bytes=56 * 1024 * 1024
        ),
        cost_estimate=pl.CostEstimate(flops=flops, bytes_accessed=24 * 1024 * 1024, transcendentals=0),
    )(matrix_settings, activations, cotangents, weights, projectors, first_moment, second_moment)


def on_device(fsdp, dp, *args):
    rank_max, settings = args[3].shape[2], args[-1]
    mats = settings.shape[0]
    widths = [w for w in range(256, rank_max, 128)] + [rank_max]
    if mats != 2 or len(widths) == 1:
        return step(fsdp, dp, (rank_max,) * mats, 0, *args)
    pairs = [(rank_max, w) for w in widths] + [(w, rank_max) for w in widths[:-1]]
    last = len(widths) - 1
    at = jnp.clip((settings[:, 0] + 127) // 128 - 2, 0, last)
    chosen = jnp.where(at[0] == last, at[1], last + 1 + at[0])
    return lax.switch(
        chosen, [functools.partial(step, fsdp, dp, pair, i) for i, pair in enumerate(pairs)], *args
    )


def solution(mesh):
    return jax.shard_map(
        functools.partial(on_device, mesh.shape["fsdp"], mesh.shape["dp"]),
        mesh=mesh,
        in_specs=(
            P(("fsdp", "dp"), None),
            P(None, ("fsdp", "dp"), None),
            P(None, "fsdp", None),
            P(None, "fsdp", None),
            P(None, "fsdp", None),
            P(None, "fsdp", None),
            P(),
        ),
        out_specs=(P(None, "fsdp", None), P(None, "fsdp", None), P(None, "fsdp", None)),
        check_vma=False,
    )
```

```python
import functools
import math

import jax
import jax.numpy as jnp
from jax import lax
from jax.experimental import pallas as pl
from jax.experimental.pallas import tpu as pltpu
from jax.sharding import PartitionSpec as P

BETA_ONE = 0.9
BETA_TWO = 0.95
EPSILON = 1e-08
MESH = pl.DeviceIdType.MESH
BF16, F32 = jnp.bfloat16, jnp.float32


def split_axis(fsdp):
    chips = fsdp // 2
    inner = 1
    while (2 * inner) ** 2 <= chips and chips % (2 * inner) == 0:
        inner *= 2
    return chips // inner, inner


def shared_rows(rows, dp):
    return (rows // 4) // 32 * 32 if dp == 2 else 0


def zone_rows(rows, dp):
    return (rows // 4) // 16 * 16 if dp == 2 else 0


def kernel(
    fsdp, dp, scale, cols,
    settings, act, cot, wts, prj, mom1, mom2, w_out, m1_out, m2_out,
    xs, proj, own_t, sib_t, send_t, own_c, sib_c, cacc, acc, zacc, yfirst, yrecv, xsend, xrecv, zsend, zrecv, ybuf, wbuf, m1, m2, nbuf,
    in_sem, out_sem, gz, gx, gy, gs, st, sc, ry0, rx, rz, ry,
):
    mats, _, rows, rank_max = proj.shape
    tokens = act.shape[0]
    outer, inner = split_axis(fsdp)
    chips = outer * inner
    me, my_dp = lax.axis_index("fsdp"), lax.axis_index("dp")
    core = lax.rem(me, 2)
    chip = me // 2
    my_x, my_z = lax.rem(chip, inner), chip // inner
    sibling = chip * 2 + 1 - core

    def chip_at(dz, dx):
        return lax.rem(my_z + dz + outer, outer) * inner + lax.rem(my_x + dx + inner, inner)

    def dev_at(dz, dx):
        return chip_at(dz, dx) * 2 + core

    sent = []

    def copy(src, dst, sems, index, device):
        return pltpu.make_async_remote_copy(
            src_ref=src,
            dst_ref=dst,
            send_sem=sems.at[(0, *index)],
            recv_sem=sems.at[(1, *index)],
            device_id=device,
            device_id_type=MESH,
        )

    def start(*args):
        one = copy(*args)
        one.start()
        sent.append(one)

    loads = [
        pltpu.make_async_copy(prj, proj.at[:, me], in_sem.at[0]),
        pltpu.make_async_copy(act, xs.at[0], in_sem.at[1]),
        pltpu.make_async_copy(cot, xs.at[pl.ds(1, mats)], in_sem.at[2]),
        pltpu.make_async_copy(mom1, m1, in_sem.at[3]),
        pltpu.make_async_copy(mom2, m2, in_sem.at[4]),
        pltpu.make_async_copy(wts, wbuf, in_sem.at[5]),
    ]
    for one in loads:
        one.start()

    partners = [{"fsdp": sibling}]
    partners += [{"fsdp": dev_at(0, e)} for e in range(1, inner)]
    partners += [{"fsdp": dev_at(d, 0)} for d in range(1, outer)]
    partners += [{"dp": lax.rem(my_dp + s, dp)} for s in range(1, dp)]
    barrier = pltpu.get_barrier_semaphore()
    for partner in partners:
        pl.semaphore_signal(barrier, inc=1, device_id=partner, device_id_type=MESH)
    pl.semaphore_wait(barrier, len(partners))
    loads[0].wait()

    share = shared_rows(rows, dp)
    window = rows - share
    half = window // 2
    window_at = my_dp * share

    def piece(k, owner, h):
        return proj.at[k, owner, pl.ds(pl.multiple_of(window_at + h * half, 16), half), pl.ds(0, cols[k])]

    def y_piece(k, owner, plane):
        return proj.at[k, owner, pl.ds(pl.multiple_of(plane * window, 16), share), pl.ds(0, cols[k])]

    def z_start(k, h):
        for d in range(1, outer):
            start(piece(k, me, h), piece(k, me, h), gz, (k, h, d - 1), {"fsdp": dev_at(d, 0)})

    def x_start(k, h, d):
        owner = dev_at(-d, 0)
        for e in range(1, inner):
            start(piece(k, owner, h), piece(k, owner, h), gx, (k, h, d, e - 1), {"fsdp": dev_at(0, e)})

    def z_forward(k, h):
        for d in range(1, outer):
            got = piece(k, dev_at(-d, 0), h)
            copy(got, got, gz, (k, h, d - 1), {"fsdp": dev_at(-d, 0)}).wait_recv()
            x_start(k, h, d)

    def y_start(k, d, e):
        if share:
            part = y_piece(k, dev_at(-d, -e), my_dp)
            start(part, part, gy, (k, d, e), {"dp": 1 - my_dp})

    def x_arrived(k, d):
        for e in range(1, inner):
            for h in range(2):
                got = piece(k, dev_at(-d, -e), h)
                copy(got, got, gx, (k, h, d, e - 1), {"fsdp": dev_at(0, -e)}).wait_recv()
            y_start(k, d, e)

    blocks = [(d, e) for e in range(inner) for d in range(outer)]

    def to_sibling(k, d, e):
        owner = dev_at(-d, -e)
        if share and (d or e):
            got = y_piece(k, owner, 1 - my_dp)
            copy(got, got, gy, (k, d, e), {"dp": 1 - my_dp}).wait_recv()
        block = proj.at[k, owner, :, pl.ds(0, cols[k])]
        start(block, block, gs, (k, d, e), {"fsdp": sibling})
        accumulate(k, owner)

    def from_sibling(k, d, e):
        owner = chip_at(-d, -e) * 2 + 1 - core
        block = proj.at[k, owner, :, pl.ds(0, cols[k])]
        copy(block, block, gs, (k, d, e), {"fsdp": sibling}).wait_recv()
        accumulate(k, owner)

    def gather(k):
        for i, at in enumerate(blocks):
            to_sibling(k, *at)
            if i:
                from_sibling(k, *blocks[i - 1])
        from_sibling(k, *blocks[-1])

    def columns(f):
        return pl.ds(pl.multiple_of(f * rows, rows), rows)

    def accumulate(k, owner):
        projected = jnp.where(settings[k, 1] == 0, 0, 1 + k)
        w = cols[k]
        cacc[k, :, :w] += jnp.dot(
            xs[projected, :, columns(owner)], proj[k, owner, :, :w], preferred_element_type=F32
        )

    z_start(0, 0)
    x_start(0, 0, 0)
    z_start(0, 1)
    x_start(0, 1, 0)

    loads[1].wait()
    loads[2].wait()

    def stage(k):
        other = jnp.where(settings[k, 1] == 0, 1 + k, 0)

        def body(c, carry):
            own_t[k, c] = xs[other, :, columns(c * 2 + core)].T
            send_t[k, c] = xs[other, :, columns(c * 2 + 1 - core)].T
            return carry

        lax.fori_loop(0, chips, body, 0)
        start(send_t.at[k], sib_t.at[k], st, (k,), {"fsdp": sibling})

    for k in range(mats):
        stage(k)
        cacc[k] = jnp.zeros((tokens, rank_max), F32)
        if k == 0:
            x_arrived(0, 0)

    z_forward(0, 0)
    z_start(1, 0)
    x_start(1, 0, 0)
    z_forward(0, 1)
    for d in range(1, outer):
        y_start(0, d, 0)
    z_start(1, 1)
    x_start(1, 1, 0)
    for d in range(1, outer):
        x_arrived(0, d)
    z_forward(1, 0)
    x_arrived(1, 0)
    for i in range(outer):
        to_sibling(0, *blocks[i])
    for i in range(outer):
        from_sibling(0, *blocks[i])
    z_forward(1, 1)
    for d in range(1, outer):
        y_start(1, d, 0)
    for i in range(outer, len(blocks)):
        to_sibling(0, *blocks[i])
        if i > outer:
            from_sibling(0, *blocks[i - 1])
    from_sibling(0, *blocks[-1])

    def coefficient_copy(k):
        part = pl.ds(0, cols[k])
        return own_c.at[k, :, part], sib_c.at[k, :, part], sc, (k,), {"fsdp": sibling}

    def coefficients(k):
        w = cols[k]
        own_c[k, :, :w] = cacc[k, :, :w].astype(BF16)
        start(*coefficient_copy(k))

    def share_arrived(k):
        copy(*coefficient_copy(k)).wait_recv()
        copy(send_t.at[k], sib_t.at[k], st, (k,), {"fsdp": sibling}).wait_recv()

    order = list(range(1, outer)) + [0]
    zone = zone_rows(rows, dp)
    span = rows - zone
    span_at = my_dp * zone
    zone_in_span = my_dp * (span - zone)

    def partial(k, c, at, size):
        part = pl.ds(pl.multiple_of(at, 16), size)
        w = cols[k]
        return jnp.dot(own_t[k, c, part], own_c[k, :, :w], preferred_element_type=F32) + jnp.dot(
            sib_t[k, c, part], sib_c[k, :, :w], preferred_element_type=F32
        )

    def zsum(k, d, e):
        ref = (yfirst.at[k, d, e, :, pl.ds(0, cols[k])], yrecv.at[k, d, e, :, pl.ds(0, cols[k])])
        return (*ref, ry0, (k, d, e), {"dp": 1 - my_dp})

    def reduce_first(k, e):
        if zone:
            for d in order:
                mine = partial(k, chip_at(d, e), (1 - my_dp) * span, zone)
                yfirst[k, d, e, :, : cols[k]] = mine.astype(BF16)
                start(*zsum(k, d, e))

    def spanned(k, d, e):
        w = cols[k]
        acc[:span, :w] = partial(k, chip_at(d, e), span_at, span)
        if zone:
            copy(*zsum(k, d, e)).wait_recv()
            acc[pl.ds(pl.multiple_of(zone_in_span, 16), zone), :w] += yrecv[k, d, e, :, :w].astype(F32)
        return acc[:span, :w]

    def x_sum(k, d, e):
        part = pl.ds(0, cols[k])
        return (
            xsend.at[k, d, e - 1, :, part], xrecv.at[k, d, e - 1, :, part], rx, (k, d, e - 1), {"fsdp": dev_at(0, e)}
        )

    def z_sum(k, d):
        part = pl.ds(0, cols[k])
        return zsend.at[k, d - 1, :, part], zrecv.at[k, d - 1, :, part], rz, (k, d - 1), {"fsdp": dev_at(d, 0)}

    def y_sum(k, s, plane):
        got = ybuf.at[k, plane, :, pl.ds(0, cols[k])]
        return got, got, ry, (k, s - 1), {"dp": lax.rem(my_dp + s, dp)}

    def reduce_x(k):
        for d in order:
            for e in range(1, inner):
                xsend[k, d, e - 1, :, : cols[k]] = spanned(k, d, e).astype(BF16)
                start(*x_sum(k, d, e))

    def reduce_z(k, d):
        w = cols[k]
        total = spanned(k, d, 0)
        for e in range(1, inner):
            copy(*x_sum(k, d, e)).wait_recv()
            total += xrecv[k, d, e - 1, :, :w].astype(F32)
        if d:
            zsend[k, d - 1, :, :w] = total.astype(BF16)
            start(*z_sum(k, d))
        else:
            zacc[k, :, :w] = total

    def reduce_y(k):
        w = cols[k]
        for d in range(1, outer):
            copy(*z_sum(k, d)).wait_recv()
        total = zacc[k, :, :w]
        for d in range(1, outer):
            total += zrecv[k, d - 1, :, :w].astype(F32)
        ybuf[k, my_dp, :, :w] = total.astype(BF16)
        for s in range(1, dp):
            start(*y_sum(k, s, my_dp))

    def finish_rows(k, at, size, terms):
        w = cols[k]
        here = pl.ds(at, size)
        total = None
        for plane, first_row in terms:
            term = ybuf[k, plane, first_row : first_row + size, :w].astype(F32)
            total = term if total is None else total + term
        live = lax.broadcasted_iota(jnp.int32, (size, w), 1) < settings[k, 0]
        grad = total * scale
        first = jnp.where(live, BETA_ONE * m1[k, here, :w] + (1.0 - BETA_ONE) * grad, 0.0)
        second = jnp.where(live, BETA_TWO * m2[k, here, :w] + (1.0 - BETA_TWO) * grad * grad, 0.0)
        m1[k, here, :w] = first
        m2[k, here, :w] = second
        nbuf[here, :w] = jnp.where(live, first / (jnp.sqrt(second) + EPSILON), 0.0).astype(BF16)

    def finish(k):
        w = cols[k]
        for s in range(1, dp):
            copy(*y_sum(k, s, lax.rem(my_dp - s + dp, dp))).wait_recv()
        if zone:
            finish_rows(k, 0, zone, [(0, 0)])
            finish_rows(k, zone, span - zone, [(0, zone), (1, 0)])
            finish_rows(k, span, zone, [(1, span - zone)])
        else:
            finish_rows(k, 0, rows, [(plane, 0) for plane in range(dp)])
        if w < rank_max:
            m1[k, :, w:] = jnp.zeros((rows, rank_max - w), F32)
            m2[k, :, w:] = jnp.zeros((rows, rank_max - w), F32)
        pltpu.make_async_copy(m1.at[k], m1_out.at[k], out_sem.at[0, k]).start()
        pltpu.make_async_copy(m2.at[k], m2_out.at[k], out_sem.at[1, k]).start()

        def body(f, carry):
            update = lax.dot_general(
                nbuf[:, :w], proj[k, f, :, :w], (((1,), (1,)), ((), ())), preferred_element_type=F32
            )
            wbuf[k, :, columns(f)] = (wbuf[k, :, columns(f)].astype(F32) - update).astype(BF16)
            return carry

        lax.fori_loop(0, fsdp, body, 0)
        pltpu.make_async_copy(wbuf.at[k], w_out.at[k], out_sem.at[2, k]).start()

    coefficients(0)
    for d in range(1, outer):
        x_arrived(1, d)
    share_arrived(0)
    for e in range(1, inner):
        reduce_first(0, e)
    reduce_x(0)
    reduce_first(0, 0)
    reduce_z(0, order[0])
    gather(1)
    coefficients(1)
    share_arrived(1)
    for e in range(1, inner):
        reduce_first(1, e)
    reduce_x(1)
    reduce_first(1, 0)
    for d in order[1:]:
        reduce_z(0, d)
    reduce_y(0)
    for d in order[:2]:
        reduce_z(1, d)
    for one in loads[3:]:
        one.wait()
    finish(0)
    for d in order[2:]:
        reduce_z(1, d)
    reduce_y(1)
    finish(1)

    for k in range(mats):
        pltpu.make_async_copy(m1.at[k], m1_out.at[k], out_sem.at[0, k]).wait()
        pltpu.make_async_copy(m2.at[k], m2_out.at[k], out_sem.at[1, k]).wait()
        pltpu.make_async_copy(wbuf.at[k], w_out.at[k], out_sem.at[2, k]).wait()
    for one in sent:
        one.wait_send()


def step(fsdp, dp, cols, number, activations, cotangents, weights, projectors, first_moment, second_moment, matrix_settings):
    tokens, features = activations.shape
    mats, rows, rank_max = projectors.shape
    outer, inner = split_axis(fsdp)
    chips = outer * inner
    zone = zone_rows(rows, dp)
    span = rows - zone
    scale = 1.0 / math.sqrt(tokens * fsdp * dp)
    hbm = pl.BlockSpec(memory_space=pl.ANY)
    sems = pltpu.SemaphoreType.DMA
    flops = 2 * mats * features * rank_max * (2 * tokens + rows) + 2 * mats * tokens * features * rank_max
    return pl.pallas_call(
        functools.partial(kernel, fsdp, dp, scale, cols),
        out_shape=(
            jax.ShapeDtypeStruct(weights.shape, weights.dtype),
            jax.ShapeDtypeStruct(first_moment.shape, first_moment.dtype),
            jax.ShapeDtypeStruct(second_moment.shape, second_moment.dtype),
        ),
        in_specs=[pl.BlockSpec(memory_space=pltpu.SMEM)] + [hbm] * 6,
        out_specs=(hbm, hbm, hbm),
        scratch_shapes=[
            pltpu.VMEM((mats + 1, tokens, features), BF16),
            pltpu.VMEM((mats, fsdp, rows, rank_max), BF16),
            pltpu.VMEM((mats, chips, rows, tokens), BF16),
            pltpu.VMEM((mats, chips, rows, tokens), BF16),
            pltpu.VMEM((mats, chips, rows, tokens), BF16),
            pltpu.VMEM((mats, tokens, rank_max), BF16),
            pltpu.VMEM((mats, tokens, rank_max), BF16),
            pltpu.VMEM((mats, tokens, rank_max), F32),
            pltpu.VMEM((rows, rank_max), F32),
            pltpu.VMEM((mats, span, rank_max), F32),
            pltpu.VMEM((mats, outer, inner, max(zone, 16), rank_max), BF16),
            pltpu.VMEM((mats, outer, inner, max(zone, 16), rank_max), BF16),
            pltpu.VMEM((mats, outer, inner - 1, span, rank_max), BF16),
            pltpu.VMEM((mats, outer, inner - 1, span, rank_max), BF16),
            pltpu.VMEM((mats, outer - 1, span, rank_max), BF16),
            pltpu.VMEM((mats, outer - 1, span, rank_max), BF16),
            pltpu.VMEM((mats, dp, span, rank_max), BF16),
            pltpu.VMEM((mats, rows, features), BF16),
            pltpu.VMEM((mats, rows, rank_max), F32),
            pltpu.VMEM((mats, rows, rank_max), F32),
            pltpu.VMEM((rows, rank_max), BF16),
            sems((6,)),
            sems((3, mats)),
            sems((2, mats, 2, outer - 1)),
            sems((2, mats, 2, outer, inner - 1)),
            sems((2, mats, outer, inner)),
            sems((2, mats, outer, inner)),
            sems((2, mats)),
            sems((2, mats)),
            sems((2, mats, outer, inner)),
            sems((2, mats, outer, inner - 1)),
            sems((2, mats, outer - 1)),
            sems((2, mats, dp - 1)),
        ],
        compiler_params=pltpu.CompilerParams(
            collective_id=number, has_side_effects=True, vmem_limit_bytes=56 * 1024 * 1024
        ),
        cost_estimate=pl.CostEstimate(flops=flops, bytes_accessed=24 * 1024 * 1024, transcendentals=0),
    )(matrix_settings, activations, cotangents, weights, projectors, first_moment, second_moment)


def on_device(fsdp, dp, *args):
    rank_max, settings = args[3].shape[2], args[-1]
    mats = settings.shape[0]
    widths = [w for w in range(256, rank_max, 128)] + [rank_max]
    if mats != 2 or len(widths) == 1:
        return step(fsdp, dp, (rank_max,) * mats, 0, *args)
    pairs = [(rank_max, w) for w in widths] + [(w, rank_max) for w in widths[:-1]]
    last = len(widths) - 1
    at = jnp.clip((settings[:, 0] + 127) // 128 - 2, 0, last)
    chosen = jnp.where(at[0] == last, at[1], last + 1 + at[0])
    return lax.switch(
        chosen, [functools.partial(step, fsdp, dp, pair, i) for i, pair in enumerate(pairs)], *args
    )


def solution(mesh):
    return jax.shard_map(
        functools.partial(on_device, mesh.shape["fsdp"], mesh.shape["dp"]),
        mesh=mesh,
        in_specs=(
            P(("fsdp", "dp"), None),
            P(None, ("fsdp", "dp"), None),
            P(None, "fsdp", None),
            P(None, "fsdp", None),
            P(None, "fsdp", None),
            P(None, "fsdp", None),
            P(),
        ),
        out_specs=(P(None, "fsdp", None), P(None, "fsdp", None), P(None, "fsdp", None)),
        check_vma=False,
    )
```
